32 devices in a mesh: groups: 2 (over x), cell: 16 (over z, y, core).
Axes of the slice: x: 2, y: 2, z: 4, core: 2. Of those that a mesh axis runs over, the one named last changes fastest.
Arguments:
- frames: bfloat16 [4096, 8, 512], P(('groups', 'cell')), parts along dimension 0
- norm_time: float32 [512], replicated, may hold values from 0.1 to 1.9
- t_wq: bfloat16 [512, 512], replicated
- t_wkv: bfloat16 [512, 1024], replicated
- t_wo: bfloat16 [512, 512], replicated, may hold values from -0.25 to 0.25
- norm_space: float32 [512], replicated, may hold values from 0.1 to 1.9
- s_wq: bfloat16 [512, 512], replicated
- s_wkv: bfloat16 [512, 1024], replicated
- s_wo: bfloat16 [512, 512], replicated, may hold values from -0.25 to 0.25
- norm_mlp: float32 [512], replicated, may hold values from 0.1 to 1.9
- w_gate: bfloat16 [512, 2048], replicated, may hold values from -0.25 to 0.25
- w_up: bfloat16 [512, 2048], replicated, may hold values from -0.25 to 0.25
- w_down: bfloat16 [2048, 512], replicated, may hold values from -0.125 to 0.125
- nbr_blocks: int32 [32, 3], P(('groups', 'cell')), parts along dimension 0, may hold values from 0 to 15, as said below
- nbr_count: int32 [32], P(('groups', 'cell')), parts along dimension 0, may hold values from 1 to 3, as said below
Outputs:
- forecast_rows: bfloat16 [4096, 8, 512], P(('groups', 'cell')), parts along dimension 0
The draws below stay inside these ranges and needn't reach their ends.
There are 2 independent parts, one for each index of `groups`. The reference program is written for one: setup_inputs(seed, part) draws one part's arguments, and reference() takes and returns one part's arrays. A program takes and returns all parts, laid end to end along the dimension named above; an argument that names none is the same for every part. Nothing has to cross between parts.
Inputs may be any that keep to these rules, and one draw needn't show every extreme that they name: `nbr_blocks`: row b lists distinct blocks b + o modulo 16 with 1 <= |o| <= 2; only the first nbr_count[b] entries of a row are used, the others are such blocks too. Block 0 lists block 15 and block 1 lists block 0, each as its first entry. `nbr_count`: some block uses all 3 entries and some block uses one.
All inputs are finite; a program needn't handle non-finite values.
Results may differ from the reference program's by a relative error of at most 0.018.
Values may be sent and summed in bfloat16 or wider, within the bound.
A program may use at most 128 MiB of HBM per device.

```python
import math
import jax
import jax.numpy as jnp
from jax import lax

D = 512
HEADS = 8
HEAD_DIM = 64
FF = 2048
TIME = 8
BLOCK = 128
NBR_MAX = 3
CELLS = 2048
BLOCKS = 16
REACH = 2
N_CELL = 16


def draw_frames(key, part):
    shape = (CELLS, TIME, D)
    return jnp.clip(jax.random.normal(key, shape, jnp.float32), -6.0, 6.0).astype(jnp.bfloat16)


def query_key(key, salt, which):
    base = jax.random.fold_in(key, salt)
    kq, kk = jax.random.split(base, 2)
    w_query = jax.random.normal(kq, (D, D), jnp.float32) / math.sqrt(D)
    w_pair = jax.random.normal(kk, (D, 2 * D), jnp.float32) / math.sqrt(D)
    if which == 0:
        return w_query
    return w_pair


def draw_t_wq(key, part):
    return query_key(key, 3, 0).astype(jnp.bfloat16)


def draw_t_wkv(key, part):
    return query_key(key, 3, 1).astype(jnp.bfloat16)


def draw_s_wq(key, part):
    return query_key(key, 5, 0).astype(jnp.bfloat16)


def draw_s_wkv(key, part):
    return query_key(key, 5, 1).astype(jnp.bfloat16)


def neighbour_lists(key):
    base = jax.random.fold_in(key, 11)
    k1, k2, k3 = jax.random.split(base, 3)
    counts = jax.random.randint(k1, (BLOCKS,), 1, NBR_MAX + 1)
    spot = jax.random.randint(k2, (), 0, BLOCKS)
    counts = counts.at[spot].set(NBR_MAX)
    counts = counts.at[(spot + 1) % BLOCKS].set(1)
    offsets = jnp.concatenate([-jnp.arange(1, REACH + 1), jnp.arange(1, REACH + 1)]).astype(jnp.int32)
    scores = jax.random.randint(k3, (BLOCKS, 2 * REACH), 0, 2 ** 20) * (2 * REACH) + jnp.arange(2 * REACH)
    scores = scores.at[0:2, 0].set(-1)
    order = jnp.argsort(scores, axis=1)[:, :NBR_MAX]
    listed = (jnp.arange(BLOCKS)[:, None] + offsets[order]) % BLOCKS
    return (listed.astype(jnp.int32), counts.astype(jnp.int32))


def draw_nbr_blocks(key, part):
    return neighbour_lists(key)[0]


def draw_nbr_count(key, part):
    return neighbour_lists(key)[1]


def noise(rng, shape, scale, most, held_as=jnp.bfloat16):
    values = jax.random.normal(rng, shape, jnp.float32) * scale
    return jnp.minimum(jnp.maximum(values, -most), most).astype(held_as)


def setup_inputs(seed: int = 0, part: int = 0) -> dict:
    key_list = jax.random.split(jax.random.key(seed), 16)
    part_keys = jax.random.split(jax.random.fold_in(key_list[15], part), 16)
    frames = draw_frames(jax.random.fold_in(jax.random.fold_in(key_list[15], part), 71), part)
    norm_time = jnp.clip(1.0 + 0.18 * jax.random.normal(key_list[1], (D,), jnp.float32), 0.1, 1.9)
    t_wq = draw_t_wq(jax.random.fold_in(key_list[15], 71), part)
    t_wkv = draw_t_wkv(jax.random.fold_in(key_list[15], 71), part)
    t_wo = noise(key_list[4], (D, D), D ** -0.5, 0.25)
    norm_space = jnp.clip(1.0 + 0.18 * jax.random.normal(key_list[5], (D,), jnp.float32), 0.1, 1.9)
    s_wq = draw_s_wq(jax.random.fold_in(key_list[15], 71), part)
    s_wkv = draw_s_wkv(jax.random.fold_in(key_list[15], 71), part)
    s_wo = noise(key_list[8], (D, D), D ** -0.5, 0.25)
    norm_mlp = jnp.clip(1.0 + 0.18 * jax.random.normal(key_list[9], (D,), jnp.float32), 0.1, 1.9)
    w_gate = noise(key_list[10], (D, FF), D ** -0.5, 0.25)
    w_up = noise(key_list[11], (D, FF), D ** -0.5, 0.25)
    w_down = noise(key_list[12], (FF, D), FF ** -0.5, 0.125)
    nbr_blocks = draw_nbr_blocks(jax.random.fold_in(jax.random.fold_in(key_list[15], part), 71), part)
    nbr_count = draw_nbr_count(jax.random.fold_in(jax.random.fold_in(key_list[15], part), 71), part)
    return {"frames": frames, "norm_time": norm_time, "t_wq": t_wq, "t_wkv": t_wkv, "t_wo": t_wo, "norm_space": norm_space, "s_wq": s_wq, "s_wkv": s_wkv, "s_wo": s_wo, "norm_mlp": norm_mlp, "w_gate": w_gate, "w_up": w_up, "w_down": w_down, "nbr_blocks": nbr_blocks, "nbr_count": nbr_count}


EPS = 1e-05

def norm_rows(rows, gain):
    wide = rows.astype(jnp.float32)
    scaled = wide * lax.rsqrt(lax.optimization_barrier(jnp.mean(wide * wide, axis=-1, keepdims=True)) + EPS)
    return (scaled * gain).astype(jnp.bfloat16)

def project_wide(rows, weight):
    lead = rows.shape[:-1]
    flat = rows.reshape(-1, rows.shape[-1])
    return jnp.dot(flat, weight, preferred_element_type=jnp.float32).reshape(lead + (weight.shape[1],))

def temporal_mix(normed, t_wq, t_wkv, t_wo):
    cells = normed.shape[0]
    query = project_wide(normed, t_wq).astype(jnp.bfloat16).reshape(cells, TIME, HEADS, HEAD_DIM)
    pairs = project_wide(normed, t_wkv).astype(jnp.bfloat16)
    keys = pairs[..., :D].reshape(cells, TIME, HEADS, HEAD_DIM)
    values = pairs[..., D:].reshape(cells, TIME, HEADS, HEAD_DIM)
    scores = jnp.einsum('cthe,cuhe->chtu', query.astype(jnp.float32), keys.astype(jnp.float32)) / math.sqrt(HEAD_DIM)
    causal = jnp.arange(TIME)[:, None] >= jnp.arange(TIME)[None, :]
    scores = jnp.where(causal, scores, -1e+30)
    probs = jax.nn.softmax(scores, axis=-1).astype(jnp.bfloat16)
    context = jnp.einsum('chtu,cuhe->cthe', probs.astype(jnp.float32), values.astype(jnp.float32)).astype(jnp.bfloat16)
    return project_wide(context.reshape(cells, TIME, D), t_wo)

def reference(frames, norm_time, t_wq, t_wkv, t_wo, norm_space, s_wq, s_wkv, s_wo, norm_mlp, w_gate, w_up, w_down, nbr_blocks, nbr_count):
    cells_all = frames.shape[0]
    normed = norm_rows(frames, norm_time)
    mixed = (frames.astype(jnp.float32) + temporal_mix(normed, t_wq, t_wkv, t_wo)).astype(jnp.bfloat16)
    per_dev = cells_all // N_CELL
    slice_cells = per_dev // N_CELL
    spaced_rows = mixed.reshape(N_CELL, N_CELL, slice_cells, TIME, D).transpose(1, 0, 2, 3, 4).reshape(cells_all, TIME, D)
    spaced_norm = norm_rows(spaced_rows, norm_space)
    query = project_wide(spaced_norm, s_wq).astype(jnp.bfloat16)
    pairs = project_wide(spaced_norm, s_wkv).astype(jnp.bfloat16)
    blocks_all = cells_all // BLOCK
    query_blocks = query.reshape(blocks_all, BLOCK, TIME, HEADS, HEAD_DIM)
    key_blocks = pairs[..., :D].reshape(blocks_all, BLOCK, TIME, HEADS, HEAD_DIM)
    value_blocks = pairs[..., D:].reshape(blocks_all, BLOCK, TIME, HEADS, HEAD_DIM)

    def one_block(item):
        block_id, own_query, listed, count = item
        picks = jnp.concatenate([block_id[None], listed]).astype(jnp.int32)
        live = jnp.concatenate([jnp.ones((1,), dtype=bool), jnp.arange(NBR_MAX) < count])
        chosen_keys = key_blocks[picks].astype(jnp.float32)
        chosen_values = value_blocks[picks].astype(jnp.float32)
        scores = jnp.einsum('qthe,skthe->thqsk', own_query.astype(jnp.float32), chosen_keys) / math.sqrt(HEAD_DIM)
        scores = jnp.where(live[None, None, None, :, None], scores, -1e+30)
        flat = scores.reshape(TIME, HEADS, BLOCK, -1)
        probs = jax.nn.softmax(flat, axis=-1).astype(jnp.bfloat16).reshape(scores.shape)
        return jnp.einsum('thqsk,skthe->qthe', probs.astype(jnp.float32), chosen_values).astype(jnp.bfloat16)
    context = lax.map(one_block, (jnp.arange(blocks_all).astype(jnp.int32), query_blocks, nbr_blocks, nbr_count))
    context = context.reshape(cells_all, TIME, D)
    after_space = (spaced_rows.astype(jnp.float32) + project_wide(context, s_wo)).astype(jnp.bfloat16)
    mlp_in = norm_rows(after_space, norm_mlp)
    hidden = (jax.nn.silu(project_wide(mlp_in, w_gate)) * project_wide(mlp_in, w_up)).astype(jnp.bfloat16)
    return (after_space.astype(jnp.float32) + project_wide(hidden, w_down)).astype(jnp.bfloat16)
```

```python
import functools
import math

import jax
import jax.numpy as jnp
from jax import lax
from jax.experimental import pallas as pl
from jax.experimental.pallas import tpu as pltpu
from jax.sharding import PartitionSpec as P

HEADS = 8
HEAD_DIM = 64
BLOCK = 128
NBR_MAX = 3
EPS = 1e-05
LANES = 128
NEG = -1e30
MESH = pl.DeviceIdType.MESH
F32 = jnp.float32
BF16 = jnp.bfloat16

GROUPS = 4
CHUNKS = 4


def norm(rows, gain):
    scaled = rows * lax.rsqrt(jnp.mean(rows * rows, axis=-1, keepdims=True) + EPS)
    return (scaled * gain).astype(BF16)


def dot(a, b):
    return jnp.dot(a, b, preferred_element_type=F32)


def dot_t(a, b):
    return lax.dot_general(a, b, (((1,), (1,)), ((), ())), preferred_element_type=F32)


def paired(query):
    low = lax.broadcasted_iota(jnp.int32, query.shape, 1) < HEAD_DIM
    zero = jnp.zeros_like(query)
    return jnp.concatenate([jnp.where(low, query, zero), jnp.where(low, zero, query)], axis=0)


def attend(query, keys, values, bias):
    rows = query.shape[0]
    scores = dot_t(paired(query), keys) + bias
    top = jnp.max(scores, axis=-1, keepdims=True)
    weights = jnp.exp(scores - top)
    total = jnp.sum(weights, axis=-1, keepdims=True)
    context = dot(weights.astype(BF16), values) / total
    low = lax.broadcasted_iota(jnp.int32, (rows, LANES), 1) < HEAD_DIM
    return jnp.where(low, context[:rows], context[rows:]).astype(BF16)


def layer(
    n, steps,
    nbr, cnt, g_time, g_space, g_mlp, frames,
    h_twq, h_twkv, h_two, h_swq, h_swkv, h_swo, h_gate, h_up, h_down,
    out,
    land, mixed, win, q, kv, ctx, outf,
    twq, twkv, two, swq, swkv, swo, gate, up, down,
    w_sem, own_sem, a_send, a_recv, n_send, n_recv,
):
    me = lax.axis_index("cell")
    width = frames.shape[-1]
    parts = width // LANES
    rows = land.shape[0] * land.shape[1]
    group_rows = rows // GROUPS
    per_group = n // GROUPS
    group_cells = group_rows // steps
    per_chunk = steps // CHUNKS
    own = 4 * BLOCK
    scale = 1.0 / math.sqrt(HEAD_DIM)

    weights = [
        pltpu.make_async_copy(src, dst, w_sem.at[i])
        for i, (src, dst) in enumerate(
            [(h_twq, twq), (h_twkv, twkv), (h_two, two), (h_swq, swq), (h_swkv, swkv),
             (h_swo, swo), (h_gate, gate), (h_up, up), (h_down, down)]
        )
    ]
    for copy in weights[:3]:
        copy.start()
    own_copy = pltpu.make_async_copy(frames.at[me], land.at[me], own_sem)
    own_copy.start()

    barrier = pltpu.get_barrier_semaphore()

    def greet(d, carry):
        pl.semaphore_signal(
            barrier, inc=1, device_id={"cell": lax.rem(me + d, n)}, device_id_type=MESH
        )
        return carry

    lax.fori_loop(1, n, greet, 0)
    pl.semaphore_wait(barrier, n - 1)

    def to_peer(d):
        dest = lax.rem(me + d, n)
        return pltpu.make_async_remote_copy(
            src_ref=frames.at[dest], dst_ref=land.at[me],
            send_sem=a_send.at[d], recv_sem=a_recv.at[d],
            device_id={"cell": dest}, device_id_type=MESH,
        )

    def send(d, carry):
        to_peer(d).start()
        return carry

    lax.fori_loop(1, n, send, 0)
    for copy in weights[3:]:
        copy.start()
    for copy in weights[:3]:
        copy.wait()
    own_copy.wait()

    first = me // per_group
    r = lax.broadcasted_iota(jnp.int32, (2 * LANES, LANES), 0) % LANES
    c = lax.broadcasted_iota(jnp.int32, (2 * LANES, LANES), 1)
    causal = jnp.where((r // steps == c // steps) & (r >= c), 0.0, NEG).astype(F32)

    def temporal(s, carry):
        g = lax.rem(first + s, GROUPS)

        def arrive(k, inner):
            src = g * per_group + k
            d = lax.rem(me - src + n, n)

            @pl.when(src != me)
            def _():
                pltpu.make_async_remote_copy(
                    src_ref=frames.at[src], dst_ref=land.at[src],
                    send_sem=a_send.at[d], recv_sem=a_recv.at[d],
                    device_id={"cell": src}, device_id_type=MESH,
                ).wait_recv()

            return inner

        lax.fori_loop(0, per_group, arrive, 0)
        x = land[pl.ds(g * per_group, per_group)].reshape(group_rows, width).astype(F32)
        normed = norm(x, g_time[...])
        tq = (dot(normed, twq[...]) * scale).astype(BF16)
        tkv = dot(normed, twkv[...]).astype(BF16)
        blocks = []
        for b in range(group_rows // LANES):
            part = slice(b * LANES, (b + 1) * LANES)
            heads = [
                attend(
                    tq[part, p * LANES : (p + 1) * LANES],
                    tkv[part, p * LANES : (p + 1) * LANES],
                    tkv[part, width + p * LANES : width + (p + 1) * LANES],
                    causal,
                )
                for p in range(parts)
            ]
            blocks.append(jnp.concatenate(heads, axis=1))
        tctx = jnp.concatenate(blocks, axis=0)
        mix = (x + dot(tctx, two[...])).astype(BF16).astype(F32)
        at = pl.multiple_of(g * group_rows, group_rows)
        for p in range(parts):
            mixed[p, pl.ds(at, group_rows), :] = mix[:, p * LANES : (p + 1) * LANES]
        cell = pl.multiple_of(own + g * group_cells, group_cells)
        for t in range(steps):
            sp = jnp.concatenate(
                [mixed[p, pl.ds(at + t, group_cells, stride=steps), :] for p in range(parts)],
                axis=1,
            )
            win[t, pl.ds(cell, group_cells), :] = norm(sp, g_space[...])
        return carry

    lax.fori_loop(0, GROUPS, temporal, 0)

    core = lax.rem(me, 2)
    side = lax.rem(me // 2, 2)
    mate = me + 1 - 2 * core
    across = me + 2 - 4 * side
    onward = lax.rem(me + n + 4 - 8 * side, n)
    last_slot = lax.rem(core + side, 2)

    def hop(kind, j, src, dst, dest):
        at = pl.ds(j * per_chunk, per_chunk)
        return pltpu.make_async_remote_copy(
            src_ref=win.at[at, pl.ds(pl.multiple_of(src * BLOCK, BLOCK), BLOCK)],
            dst_ref=win.at[at, pl.ds(dst * BLOCK, BLOCK)],
            send_sem=n_send.at[kind, j], recv_sem=n_recv.at[kind, j],
            device_id={"cell": dest}, device_id_type=MESH,
        )

    def hop_across(j):
        return hop(0, j, 4, 0, across)

    def hop_onward(j):
        return hop(1, j, 0, 1, onward)

    def hop_mate(j):
        return hop(2, j, 4, 2, mate)

    def hop_last(j):
        return hop(3, j, last_slot, 3, mate)

    def send_own(j, carry):
        hop_across(j).start()
        hop_mate(j).start()
        return carry

    lax.fori_loop(0, CHUNKS, send_own, 0)
    for copy in weights[3:]:
        copy.wait()

    def own_pairs(j, carry):
        t = j * per_chunk
        sn = win[pl.ds(t, per_chunk), pl.ds(own, BLOCK), :].reshape(per_chunk * BLOCK, width)
        q[pl.ds(t, per_chunk)] = (
            (dot(sn, swq[...]) * scale).astype(BF16).reshape(per_chunk, BLOCK, width)
        )
        kv[pl.ds(t, per_chunk), pl.ds(own, BLOCK), :] = (
            dot(sn, swkv[...]).astype(BF16).reshape(per_chunk, BLOCK, 2 * width)
        )
        return carry

    lax.fori_loop(0, CHUNKS, own_pairs, 0)

    for j in range(2):
        hop_across(j).wait_recv()
        hop_onward(j).start()
    hop_onward(0).wait_recv()
    hop_last(0).start()

    chip = me // 2
    adjacent = lax.rem(chip + n // 2 - 1 + 2 * side, n // 2)
    ids = [across, 2 * adjacent + core, mate, lax.rem(me + n - 1 + 2 * core, n)]
    biases = []
    for block in ids:
        hit = jnp.int32(0)
        for j in range(NBR_MAX):
            hit = hit + jnp.where((nbr[0, j] == block) & (j < cnt[0]), 1, 0)
        biases.append(jnp.full((1, BLOCK), jnp.where(hit > 0, 0.0, NEG), F32))
    biases.append(jnp.zeros((1, BLOCK), F32))
    bias = jnp.concatenate(biases, axis=1)

    def chunk(j, carry):
        hop_mate(j).wait_recv()
        hop_last(j).wait_recv()

        def spatial(k, inner):
            t = j * per_chunk + k
            kv[t, pl.ds(0, own), :] = dot(win[t, pl.ds(0, own), :], swkv[...]).astype(BF16)
            for p in range(parts):
                lanes = slice(p * LANES, (p + 1) * LANES)
                ctx[k, :, lanes] = attend(
                    q[t, :, lanes], kv[t, :, lanes],
                    kv[t, :, width + p * LANES : width + (p + 1) * LANES], bias,
                )
            return inner

        lax.fori_loop(0, per_chunk, spatial, 0)

        @pl.when(j + 2 < CHUNKS)
        def _():
            hop_across(j + 2).wait_recv()
            hop_onward(j + 2).start()

        @pl.when(j + 1 < CHUNKS)
        def _():
            hop_onward(j + 1).wait_recv()
            hop_last(j + 1).start()

        spaced = jnp.concatenate(
            [
                jnp.concatenate(
                    [mixed[p, pl.ds(j * per_chunk + k, BLOCK, stride=steps), :] for p in range(parts)],
                    axis=1,
                )
                for k in range(per_chunk)
            ],
            axis=0,
        )
        after = (spaced + dot(ctx[...].reshape(per_chunk * BLOCK, width), swo[...])).astype(BF16)
        after = after.astype(F32)
        mn = norm(after, g_mlp[...])
        total = after
        hidden_width = gate.shape[1]
        piece = min(512, hidden_width)
        for f in range(0, hidden_width, piece):
            v = dot(mn, gate[:, f : f + piece])
            u = dot(mn, up[:, f : f + piece])
            hidden = (v / (1.0 + jnp.exp(-v)) * u).astype(BF16)
            total = total + dot(hidden, down[f : f + piece, :])
        for k in range(per_chunk):
            for p in range(parts):
                outf[p, pl.ds(j * per_chunk + k, BLOCK, stride=steps), :] = total[
                    k * BLOCK : (k + 1) * BLOCK, p * LANES : (p + 1) * LANES
                ]
        return carry

    lax.fori_loop(0, CHUNKS, chunk, 0)

    for p in range(parts):
        out[:, p * LANES : (p + 1) * LANES] = outf[p].astype(BF16)

    def drain(d, carry):
        to_peer(d).wait_send()
        return carry

    lax.fori_loop(1, n, drain, 0)

    def drain_hops(j, carry):
        hop_across(j).wait_send()
        hop_onward(j).wait_send()
        hop_mate(j).wait_send()
        hop_last(j).wait_send()
        return carry

    lax.fori_loop(0, CHUNKS, drain_hops, 0)


def per_device(
    frames, norm_time, t_wq, t_wkv, t_wo, norm_space, s_wq, s_wkv, s_wo, norm_mlp,
    w_gate, w_up, w_down, nbr_blocks, nbr_count,
):
    n = lax.axis_size("cell")
    cells, steps, width = frames.shape
    rows = cells * steps
    hidden = w_gate.shape[1]
    parts = width // LANES
    smem = pl.BlockSpec(memory_space=pltpu.SMEM)
    vmem = pl.BlockSpec(memory_space=pltpu.VMEM)
    anyw = pl.BlockSpec(memory_space=pl.ANY)
    weights = [t_wq, t_wkv, t_wo, s_wq, s_wkv, s_wo, w_gate, w_up, w_down]
    out = pl.pallas_call(
        functools.partial(layer, n, steps),
        out_shape=jax.ShapeDtypeStruct((rows, width), BF16),
        in_specs=[smem, smem, vmem, vmem, vmem, anyw] + [anyw] * len(weights),
        out_specs=vmem,
        scratch_shapes=[
            pltpu.VMEM((n, rows // n, width), BF16),
            pltpu.VMEM((parts, rows, LANES), F32),
            pltpu.VMEM((steps, 5 * BLOCK, width), BF16),
            pltpu.VMEM((steps, BLOCK, width), BF16),
            pltpu.VMEM((steps, 5 * BLOCK, 2 * width), BF16),
            pltpu.VMEM((steps // CHUNKS, BLOCK, width), BF16),
            pltpu.VMEM((parts, rows, LANES), F32),
        ]
        + [pltpu.VMEM(w.shape, BF16) for w in weights]
        + [
            pltpu.SemaphoreType.DMA((len(weights),)),
            pltpu.SemaphoreType.DMA,
            pltpu.SemaphoreType.DMA((n,)),
            pltpu.SemaphoreType.DMA((n,)),
            pltpu.SemaphoreType.DMA((4, CHUNKS)),
            pltpu.SemaphoreType.DMA((4, CHUNKS)),
        ],
        compiler_params=pltpu.CompilerParams(
            collective_id=0, has_side_effects=True, vmem_limit_bytes=56 * 1024 * 1024
        ),
        cost_estimate=pl.CostEstimate(
            flops=2 * rows * width * (12 * width + 3 * hidden), bytes_accessed=14 * 2**20,
            transcendentals=rows * 5 * BLOCK * HEADS,
        ),
    )(
        nbr_blocks, nbr_count, norm_time[None], norm_space[None], norm_mlp[None],
        frames.reshape(n, rows // n, width), *weights,
    )
    return out.reshape(cells, steps, width)


def solution(mesh):
    split3 = P(("groups", "cell"), None, None)
    placed = (split3,) + (P(),) * 12 + (P(("groups", "cell"), None), P(("groups", "cell")))
    return jax.shard_map(
        per_device, mesh=mesh, in_specs=placed, out_specs=split3, check_vma=False
    )
```

```python
import functools
import math

import jax
import jax.numpy as jnp
from jax import lax
from jax.experimental import pallas as pl
from jax.experimental.pallas import tpu as pltpu
from jax.sharding import PartitionSpec as P

HEADS = 8
HEAD_DIM = 64
BLOCK = 128
NBR_MAX = 3
EPS = 1e-05
LANES = 128
NEG = -1e30
MESH = pl.DeviceIdType.MESH
F32 = jnp.float32
BF16 = jnp.bfloat16

GROUPS = 4
CHUNKS = 4


def norm(rows, gain):
    scaled = rows * lax.rsqrt(jnp.mean(rows * rows, axis=-1, keepdims=True) + EPS)
    return (scaled * gain).astype(BF16)


def dot(a, b):
    return jnp.dot(a, b, preferred_element_type=F32)


def dot_t(a, b):
    return lax.dot_general(a, b, (((1,), (1,)), ((), ())), preferred_element_type=F32)


def paired(query):
    low = lax.broadcasted_iota(jnp.int32, query.shape, 1) < HEAD_DIM
    zero = jnp.zeros_like(query)
    return jnp.concatenate([jnp.where(low, query, zero), jnp.where(low, zero, query)], axis=0)


def attend(query, keys, values, bias):
    rows = query.shape[0]
    scores = dot_t(paired(query), keys) + bias
    top = jnp.max(scores, axis=-1, keepdims=True)
    weights = jnp.exp(scores - top)
    total = jnp.sum(weights, axis=-1, keepdims=True)
    context = dot(weights.astype(BF16), values) / total
    low = lax.broadcasted_iota(jnp.int32, (rows, LANES), 1) < HEAD_DIM
    return jnp.where(low, context[:rows], context[rows:]).astype(BF16)


def layer(
    n, steps,
    nbr, cnt, g_time, g_space, g_mlp, frames,
    h_twq, h_twkv, h_two, h_swq, h_swkv, h_swo, h_gate, h_up, h_down,
    out,
    land, mixed, win, q, kv, ctx, outf,
    twq, twkv, two, swq, swkv, swo, gate, up, down,
    w_sem, own_sem, a_send, a_recv, f_send, f_recv, n_send, n_recv,
):
    me = lax.axis_index("cell")
    width = frames.shape[-1]
    parts = width // LANES
    planes = n // 4
    half = n // 2
    rows = mixed.shape[2]
    group_rows = rows // GROUPS
    per_group = planes // GROUPS
    group_cells = group_rows // steps
    per_chunk = steps // CHUNKS
    got = 3 * BLOCK
    own = 4 * BLOCK
    scale = 1.0 / math.sqrt(HEAD_DIM)

    plane = me // 4
    side = lax.rem(me // 2, 2)
    core = lax.rem(me, 2)
    spot = 2 * plane + core
    across = me + 2 - 4 * side
    mate = me + 1 - 2 * core

    weights = [
        pltpu.make_async_copy(src, dst, w_sem.at[i])
        for i, (src, dst) in enumerate(
            [(h_twq, twq), (h_twkv, twkv), (h_two, two), (h_swq, swq), (h_swkv, swkv),
             (h_swo, swo), (h_gate, gate), (h_up, up), (h_down, down)]
        )
    ]
    for copy in weights[:3]:
        copy.start()
    own_copy = pltpu.make_async_copy(
        frames.at[plane, :, core], land.at[:, plane, side, core], own_sem
    )
    own_copy.start()

    def same_side(at):
        return 4 * (at // 2) + 2 * side + lax.rem(at, 2)

    barrier = pltpu.get_barrier_semaphore()

    def greet(d, carry):
        peer = same_side(lax.rem(spot + d, half))
        pl.semaphore_signal(barrier, inc=1, device_id={"cell": peer}, device_id_type=MESH)
        return carry

    lax.fori_loop(1, half, greet, 0)
    pl.semaphore_signal(barrier, inc=1, device_id={"cell": across}, device_id_type=MESH)
    pl.semaphore_wait(barrier, half)

    def to_peer(d):
        at = lax.rem(spot + d, half)
        return pltpu.make_async_remote_copy(
            src_ref=frames.at[at // 2, :, lax.rem(at, 2)],
            dst_ref=land.at[:, plane, side, core],
            send_sem=a_send.at[d], recv_sem=a_recv.at[d],
            device_id={"cell": same_side(at)}, device_id_type=MESH,
        )

    def send(d, carry):
        to_peer(d).start()
        return carry

    lax.fori_loop(1, half, send, 0)
    for copy in weights[3:]:
        copy.start()
    for copy in weights[:3]:
        copy.wait()
    own_copy.wait()

    first = plane // per_group
    r = lax.broadcasted_iota(jnp.int32, (2 * LANES, LANES), 0) % LANES
    c = lax.broadcasted_iota(jnp.int32, (2 * LANES, LANES), 1)
    causal = jnp.where((r // steps == c // steps) & (r >= c), 0.0, NEG).astype(F32)

    def group_at(e):
        return lax.rem(first - e + GROUPS, GROUPS)

    def pass_across(e):
        block = land.at[:, pl.ds(group_at(e) * per_group, per_group), side]
        return pltpu.make_async_remote_copy(
            src_ref=block, dst_ref=block, send_sem=f_send.at[e], recv_sem=f_recv.at[e],
            device_id={"cell": across}, device_id_type=MESH,
        )

    def arrive(e):
        def one(i, inner):
            at = group_at(e) * 2 * per_group + i

            @pl.when(at != spot)
            def _():
                d = lax.rem(spot - at + half, half)
                pltpu.make_async_remote_copy(
                    src_ref=frames.at[0, :, 0], dst_ref=land.at[:, at // 2, side, lax.rem(at, 2)],
                    send_sem=a_send.at[d], recv_sem=a_recv.at[d],
                    device_id={"cell": same_side(at)}, device_id_type=MESH,
                ).wait_recv()

            return inner

        lax.fori_loop(0, 2 * per_group, one, 0)
        pass_across(e).start()

    arrive(0)

    def temporal(e, carry):
        g = group_at(e)

        @pl.when(e + 1 < GROUPS)
        def _():
            arrive(e + 1)

        pass_across(e).wait_recv()
        x = land[:, pl.ds(g * per_group, per_group)].reshape(2 * group_rows, width).astype(F32)
        normed = norm(x, g_time[...])
        tq = (dot(normed, twq[...]) * scale).astype(BF16)
        tkv = dot(normed, twkv[...]).astype(BF16)
        blocks = []
        for b in range(2 * group_rows // LANES):
            part = slice(b * LANES, (b + 1) * LANES)
            heads = [
                attend(
                    tq[part, p * LANES : (p + 1) * LANES],
                    tkv[part, p * LANES : (p + 1) * LANES],
                    tkv[part, width + p * LANES : width + (p + 1) * LANES],
                    causal,
                )
                for p in range(parts)
            ]
            blocks.append(jnp.concatenate(heads, axis=1))
        tctx = jnp.concatenate(blocks, axis=0)
        mix = (x + dot(tctx, two[...])).astype(BF16).astype(F32)
        at = pl.multiple_of(g * group_rows, group_rows)
        for b in range(2):
            for p in range(parts):
                mixed[b, p, pl.ds(at, group_rows), :] = mix[
                    b * group_rows : (b + 1) * group_rows, p * LANES : (p + 1) * LANES
                ]
            slot = jnp.where(side == b, 4, 3)
            cell = pl.multiple_of(slot * BLOCK + g * group_cells, group_cells)
            for t in range(steps):
                sp = jnp.concatenate(
                    [
                        mixed[b, p, pl.ds(at + t, group_cells, stride=steps), :]
                        for p in range(parts)
                    ],
                    axis=1,
                )
                win[t, pl.ds(cell, group_cells), :] = norm(sp, g_space[...])
        return carry

    lax.fori_loop(0, GROUPS, temporal, 0)

    onward = lax.rem(me + n + 4 - 8 * side, n)
    has_last = core == side
    last_slot = jnp.where(has_last, 3, 0)

    def hop(kind, j, src, dst, dest):
        at = pl.ds(j * per_chunk, per_chunk)
        return pltpu.make_async_remote_copy(
            src_ref=win.at[at, pl.ds(pl.multiple_of(src * BLOCK, BLOCK), BLOCK)],
            dst_ref=win.at[at, pl.ds(dst * BLOCK, BLOCK)],
            send_sem=n_send.at[kind, j], recv_sem=n_recv.at[kind, j],
            device_id={"cell": dest}, device_id_type=MESH,
        )

    def hop_onward(j):
        return hop(0, j, 3, 0, onward)

    def hop_mate(j):
        return hop(1, j, 4, 1, mate)

    def hop_last(j):
        return hop(2, j, last_slot, 2, mate)

    def send_own(j, carry):
        hop_onward(j).start()
        hop_mate(j).start()

        @pl.when(has_last)
        def _():
            hop_last(j).start()

        return carry

    def relay(j):
        hop_onward(j).wait_recv()

        @pl.when(jnp.logical_not(has_last))
        def _():
            hop_last(j).start()

    lax.fori_loop(0, CHUNKS, send_own, 0)
    for copy in weights[3:]:
        copy.wait()

    def own_pairs(j, carry):
        t = j * per_chunk
        sn = win[pl.ds(t, per_chunk), pl.ds(own, BLOCK), :].reshape(per_chunk * BLOCK, width)
        q[pl.ds(t, per_chunk)] = (
            (dot(sn, swq[...]) * scale).astype(BF16).reshape(per_chunk, BLOCK, width)
        )
        sn = win[pl.ds(t, per_chunk), pl.ds(got, 2 * BLOCK), :]
        kv[pl.ds(t, per_chunk), pl.ds(got, 2 * BLOCK), :] = (
            dot(sn.reshape(per_chunk * 2 * BLOCK, width), swkv[...])
            .astype(BF16).reshape(per_chunk, 2 * BLOCK, 2 * width)
        )
        return carry

    lax.fori_loop(0, CHUNKS, own_pairs, 0)

    relay(0)

    chip = me // 2
    adjacent = lax.rem(chip + n // 2 - 1 + 2 * side, n // 2)
    ids = [2 * adjacent + core, mate, lax.rem(me + n - 1 + 2 * core, n), across]
    biases = []
    for block in ids:
        hit = jnp.int32(0)
        for j in range(NBR_MAX):
            hit = hit + jnp.where((nbr[0, j] == block) & (j < cnt[0]), 1, 0)
        biases.append(jnp.full((1, BLOCK), jnp.where(hit > 0, 0.0, NEG), F32))
    biases.append(jnp.zeros((1, BLOCK), F32))
    bias = jnp.concatenate(biases, axis=1)

    def chunk(j, carry):
        hop_mate(j).wait_recv()
        hop_last(j).wait_recv()

        def spatial(k, inner):
            t = j * per_chunk + k
            kv[t, pl.ds(0, got), :] = dot(win[t, pl.ds(0, got), :], swkv[...]).astype(BF16)
            for p in range(parts):
                lanes = slice(p * LANES, (p + 1) * LANES)
                ctx[k, :, lanes] = attend(
                    q[t, :, lanes], kv[t, :, lanes],
                    kv[t, :, width + p * LANES : width + (p + 1) * LANES], bias,
                )
            return inner

        lax.fori_loop(0, per_chunk, spatial, 0)

        @pl.when(j + 1 < CHUNKS)
        def _():
            relay(j + 1)

        spaced = jnp.concatenate(
            [
                jnp.concatenate(
                    [
                        mixed[side, p, pl.ds(j * per_chunk + k, BLOCK, stride=steps), :]
                        for p in range(parts)
                    ],
                    axis=1,
                )
                for k in range(per_chunk)
            ],
            axis=0,
        )
        after = (spaced + dot(ctx[...].reshape(per_chunk * BLOCK, width), swo[...])).astype(BF16)
        after = after.astype(F32)
        mn = norm(after, g_mlp[...])
        total = after
        hidden_width = gate.shape[1]
        piece = min(512, hidden_width)
        for f in range(0, hidden_width, piece):
            v = dot(mn, gate[:, f : f + piece])
            u = dot(mn, up[:, f : f + piece])
            hidden = (v / (1.0 + jnp.exp(-v)) * u).astype(BF16)
            total = total + dot(hidden, down[f : f + piece, :])
        for k in range(per_chunk):
            for p in range(parts):
                outf[p, pl.ds(j * per_chunk + k, BLOCK, stride=steps), :] = total[
                    k * BLOCK : (k + 1) * BLOCK, p * LANES : (p + 1) * LANES
                ]
        return carry

    lax.fori_loop(0, CHUNKS, chunk, 0)

    for p in range(parts):
        out[:, p * LANES : (p + 1) * LANES] = outf[p].astype(BF16)

    def drain(d, carry):
        to_peer(d).wait_send()
        return carry

    lax.fori_loop(1, half, drain, 0)

    def drain_across(e, carry):
        pass_across(e).wait_send()
        return carry

    lax.fori_loop(0, GROUPS, drain_across, 0)

    def drain_hops(j, carry):
        hop_onward(j).wait_send()
        hop_mate(j).wait_send()
        hop_last(j).wait_send()
        return carry

    lax.fori_loop(0, CHUNKS, drain_hops, 0)


def per_device(
    frames, norm_time, t_wq, t_wkv, t_wo, norm_space, s_wq, s_wkv, s_wo, norm_mlp,
    w_gate, w_up, w_down, nbr_blocks, nbr_count,
):
    n = lax.axis_size("cell")
    cells, steps, width = frames.shape
    rows = cells * steps
    hidden = w_gate.shape[1]
    parts = width // LANES
    smem = pl.BlockSpec(memory_space=pltpu.SMEM)
    vmem = pl.BlockSpec(memory_space=pltpu.VMEM)
    anyw = pl.BlockSpec(memory_space=pl.ANY)
    weights = [t_wq, t_wkv, t_wo, s_wq, s_wkv, s_wo, w_gate, w_up, w_down]
    out = pl.pallas_call(
        functools.partial(layer, n, steps),
        out_shape=jax.ShapeDtypeStruct((rows, width), BF16),
        in_specs=[smem, smem, vmem, vmem, vmem, anyw] + [anyw] * len(weights),
        out_specs=vmem,
        scratch_shapes=[
            pltpu.VMEM((2, n // 4, 2, 2, rows // n, width), BF16),
            pltpu.VMEM((2, parts, rows, LANES), F32),
            pltpu.VMEM((steps, 5 * BLOCK, width), BF16),
            pltpu.VMEM((steps, BLOCK, width), BF16),
            pltpu.VMEM((steps, 5 * BLOCK, 2 * width), BF16),
            pltpu.VMEM((steps // CHUNKS, BLOCK, width), BF16),
            pltpu.VMEM((parts, rows, LANES), F32),
        ]
        + [pltpu.VMEM(w.shape, BF16) for w in weights]
        + [
            pltpu.SemaphoreType.DMA((len(weights),)),
            pltpu.SemaphoreType.DMA,
            pltpu.SemaphoreType.DMA((n // 2,)),
            pltpu.SemaphoreType.DMA((n // 2,)),
            pltpu.SemaphoreType.DMA((GROUPS,)),
            pltpu.SemaphoreType.DMA((GROUPS,)),
            pltpu.SemaphoreType.DMA((3, CHUNKS)),
            pltpu.SemaphoreType.DMA((3, CHUNKS)),
        ],
        compiler_params=pltpu.CompilerParams(
            collective_id=0, has_side_effects=True, vmem_limit_bytes=56 * 1024 * 1024
        ),
        cost_estimate=pl.CostEstimate(
            flops=2 * rows * width * (12 * width + 3 * hidden), bytes_accessed=14 * 2**20,
            transcendentals=rows * 5 * BLOCK * HEADS,
        ),
    )(
        nbr_blocks, nbr_count, norm_time[None], norm_space[None], norm_mlp[None],
        frames.reshape(n // 4, 2, 2, rows // n, width), *weights,
    )
    return out.reshape(cells, steps, width)


def solution(mesh):
    split3 = P(("groups", "cell"), None, None)
    placed = (split3,) + (P(),) * 12 + (P(("groups", "cell"), None), P(("groups", "cell")))
    return jax.shard_map(
        per_device, mesh=mesh, in_specs=placed, out_specs=split3, check_vma=False
    )
```

```python
import functools
import math

import jax
import jax.numpy as jnp
from jax import lax
from jax.experimental import pallas as pl
from jax.experimental.pallas import tpu as pltpu
from jax.sharding import PartitionSpec as P

HEADS = 8
HEAD_DIM = 64
BLOCK = 128
NBR_MAX = 3
EPS = 1e-05
LANES = 128
NEG = -1e30
MESH = pl.DeviceIdType.MESH
F32 = jnp.float32
BF16 = jnp.bfloat16

GROUPS = 4
CHUNKS = 4


def norm(rows, gain):
    scaled = rows * lax.rsqrt(jnp.mean(rows * rows, axis=-1, keepdims=True) + EPS)
    return (scaled * gain).astype(BF16)


def dot(a, b):
    return jnp.dot(a, b, preferred_element_type=F32)


def dot_t(a, b):
    return lax.dot_general(a, b, (((1,), (1,)), ((), ())), preferred_element_type=F32)


def paired(query):
    low = lax.broadcasted_iota(jnp.int32, query.shape, 1) < HEAD_DIM
    zero = jnp.zeros_like(query)
    return jnp.concatenate([jnp.where(low, query, zero), jnp.where(low, zero, query)], axis=0)


def attend(query, keys, values, bias):
    rows = query.shape[0]
    scores = dot_t(paired(query), keys) + bias
    top = jnp.max(scores, axis=-1, keepdims=True)
    weights = jnp.exp2(scores - top)
    low = lax.broadcasted_iota(jnp.int32, (rows, LANES), 1) < HEAD_DIM
    if values.shape[0] == LANES:
        total = jnp.sum(weights, axis=-1, keepdims=True)
        both = dot(weights.astype(BF16), values) * pl.reciprocal(total, approx=True)
        return jnp.where(low, both[:rows], both[rows:]).astype(BF16)
    ones = jnp.ones((values.shape[0], LANES), BF16)
    both = dot(weights.astype(BF16), jnp.concatenate([values, ones], axis=1))
    mixed = jnp.where(low, both[:rows, :LANES], both[rows:, :LANES])
    total = jnp.where(low, both[:rows, LANES:], both[rows:, LANES:])
    return (mixed * pl.reciprocal(total, approx=True)).astype(BF16)


def layer(
    n, steps,
    nbr, cnt, g_time, g_space, g_mlp, frames,
    h_twq, h_twkv, h_two, h_swq, h_swkv, h_swo, h_gate, h_up, h_down,
    out,
    land, mixed, win, q, kv, ctx, outf,
    twq, twkv, two, swq, swkv, swo, gate, up, down,
    w_sem, own_sem, a_send, a_recv, f_send, f_recv, n_send, n_recv,
):
    me = lax.axis_index("cell")
    width = frames.shape[-1]
    parts = width // LANES
    planes = n // 4
    half = n // 2
    rows = mixed.shape[2]
    group_rows = rows // GROUPS
    per_group = planes // GROUPS
    group_cells = group_rows // steps
    per_chunk = steps // CHUNKS
    got = 3 * BLOCK
    own = 4 * BLOCK
    scale = math.log2(math.e) / math.sqrt(HEAD_DIM)

    plane = me // 4
    side = lax.rem(me // 2, 2)
    core = lax.rem(me, 2)
    spot = 2 * plane + core
    across = me + 2 - 4 * side
    mate = me + 1 - 2 * core

    weights = [
        pltpu.make_async_copy(src, dst, w_sem.at[i])
        for i, (src, dst) in enumerate(
            [(h_twq, twq), (h_twkv, twkv), (h_two, two), (h_swq, swq), (h_swkv, swkv),
             (h_swo, swo), (h_gate, gate), (h_up, up), (h_down, down)]
        )
    ]
    for copy in weights[:3]:
        copy.start()
    own_copy = pltpu.make_async_copy(
        frames.at[plane, :, core], land.at[:, plane, side, core], own_sem
    )
    own_copy.start()

    def same_side(at):
        return 4 * (at // 2) + 2 * side + lax.rem(at, 2)

    barrier = pltpu.get_barrier_semaphore()

    def greet(d, carry):
        peer = same_side(lax.rem(spot + d, half))
        pl.semaphore_signal(barrier, inc=1, device_id={"cell": peer}, device_id_type=MESH)
        return carry

    lax.fori_loop(1, half, greet, 0)
    pl.semaphore_signal(barrier, inc=1, device_id={"cell": across}, device_id_type=MESH)
    pl.semaphore_wait(barrier, half)

    def to_peer(d):
        at = lax.rem(spot + d, half)
        return pltpu.make_async_remote_copy(
            src_ref=frames.at[at // 2, :, lax.rem(at, 2)],
            dst_ref=land.at[:, plane, side, core],
            send_sem=a_send.at[d], recv_sem=a_recv.at[d],
            device_id={"cell": same_side(at)}, device_id_type=MESH,
        )

    first = plane // per_group

    def group_at(e):
        low = lax.rem(lax.rem(first, 2) + lax.rem(jnp.int32(e), 2), 2)
        return 2 * lax.rem(first // 2 + jnp.int32(e) // 2, 2) + low

    def send_group(e):
        def one(i, carry):
            at = group_at(e) * 2 * per_group + i

            @pl.when(at != spot)
            def _():
                to_peer(lax.rem(at - spot + half, half)).start()

            return carry

        lax.fori_loop(0, 2 * per_group, one, 0)

    for e in (0, 2, 1):
        send_group(e)
    for copy in weights[3:]:
        copy.start()
    for copy in weights[:3]:
        copy.wait()
    own_copy.wait()

    r = lax.broadcasted_iota(jnp.int32, (2 * LANES, LANES), 0) % LANES
    c = lax.broadcasted_iota(jnp.int32, (2 * LANES, LANES), 1)
    causal = jnp.where((r // steps == c // steps) & (r >= c), 0.0, NEG).astype(F32)

    def pass_across(e):
        block = land.at[:, pl.ds(group_at(e) * per_group, per_group), side]
        return pltpu.make_async_remote_copy(
            src_ref=block, dst_ref=block, send_sem=f_send.at[e], recv_sem=f_recv.at[e],
            device_id={"cell": across}, device_id_type=MESH,
        )

    def arrive(e):
        def one(i, inner):
            at = group_at(e) * 2 * per_group + i

            @pl.when(at != spot)
            def _():
                d = lax.rem(spot - at + half, half)
                pltpu.make_async_remote_copy(
                    src_ref=frames.at[0, :, 0], dst_ref=land.at[:, at // 2, side, lax.rem(at, 2)],
                    send_sem=a_send.at[d], recv_sem=a_recv.at[d],
                    device_id={"cell": same_side(at)}, device_id_type=MESH,
                ).wait_recv()

            return inner

        lax.fori_loop(0, 2 * per_group, one, 0)
        pass_across(e).start()

    arrive(0)
    arrive(1)
    send_group(3)

    def temporal(e, carry):
        g = group_at(e)

        @pl.when(e + 2 < GROUPS)
        def _():
            arrive(e + 2)

        pass_across(e).wait_recv()
        x = land[:, pl.ds(g * per_group, per_group)].reshape(2 * group_rows, width).astype(F32)
        normed = norm(x, g_time[...])
        tq = (dot(normed, twq[...]) * scale).astype(BF16)
        tkv = dot(normed, twkv[...]).astype(BF16)
        blocks = []
        for b in range(2 * group_rows // LANES):
            part = slice(b * LANES, (b + 1) * LANES)
            heads = [
                attend(
                    tq[part, p * LANES : (p + 1) * LANES],
                    tkv[part, p * LANES : (p + 1) * LANES],
                    tkv[part, width + p * LANES : width + (p + 1) * LANES],
                    causal,
                )
                for p in range(parts)
            ]
            blocks.append(jnp.concatenate(heads, axis=1))
        tctx = jnp.concatenate(blocks, axis=0)
        mix = (x + dot(tctx, two[...])).astype(BF16).astype(F32)
        at = pl.multiple_of(g * group_rows, group_rows)
        for b in range(2):
            for p in range(parts):
                mixed[b, p, pl.ds(at, group_rows), :] = mix[
                    b * group_rows : (b + 1) * group_rows, p * LANES : (p + 1) * LANES
                ]
            slot = jnp.where(side == b, 4, 3)
            cell = pl.multiple_of(slot * BLOCK + g * group_cells, group_cells)
            for t in range(steps):
                sp = jnp.concatenate(
                    [
                        mixed[b, p, pl.ds(at + t, group_cells, stride=steps), :]
                        for p in range(parts)
                    ],
                    axis=1,
                )
                win[t, pl.ds(cell, group_cells), :] = norm(sp, g_space[...])
        return carry

    lax.fori_loop(0, GROUPS, temporal, 0)

    onward = lax.rem(me + n + 4 - 8 * side, n)
    has_last = core == side
    last_slot = jnp.where(has_last, 3, 0)

    def hop(kind, j, src, dst, dest):
        at = pl.ds(j * per_chunk, per_chunk)
        return pltpu.make_async_remote_copy(
            src_ref=win.at[at, pl.ds(pl.multiple_of(src * BLOCK, BLOCK), BLOCK)],
            dst_ref=win.at[at, pl.ds(dst * BLOCK, BLOCK)],
            send_sem=n_send.at[kind, j], recv_sem=n_recv.at[kind, j],
            device_id={"cell": dest}, device_id_type=MESH,
        )

    def hop_onward(j):
        return hop(0, j, 3, 0, onward)

    def hop_mate(j):
        return hop(1, j, 4, 1, mate)

    def hop_last(j):
        return hop(2, j, last_slot, 2, mate)

    def send_own(j, carry):
        hop_onward(j).start()
        hop_mate(j).start()

        @pl.when(has_last)
        def _():
            hop_last(j).start()

        return carry

    def relay(j):
        hop_onward(j).wait_recv()

        @pl.when(jnp.logical_not(has_last))
        def _():
            hop_last(j).start()

    lax.fori_loop(0, CHUNKS, send_own, 0)
    for copy in weights[3:]:
        copy.wait()

    def own_pairs(j, carry):
        t = j * per_chunk
        sn = win[pl.ds(t, per_chunk), pl.ds(own, BLOCK), :].reshape(per_chunk * BLOCK, width)
        q[pl.ds(t, per_chunk)] = (
            (dot(sn, swq[...]) * scale).astype(BF16).reshape(per_chunk, BLOCK, width)
        )
        sn = win[pl.ds(t, per_chunk), pl.ds(got, 2 * BLOCK), :]
        kv[pl.ds(t, per_chunk), pl.ds(got, 2 * BLOCK), :] = (
            dot(sn.reshape(per_chunk * 2 * BLOCK, width), swkv[...])
            .astype(BF16).reshape(per_chunk, 2 * BLOCK, 2 * width)
        )
        return carry

    lax.fori_loop(0, CHUNKS, own_pairs, 0)

    relay(0)

    chip = me // 2
    adjacent = lax.rem(chip + n // 2 - 1 + 2 * side, n // 2)
    ids = [2 * adjacent + core, mate, lax.rem(me + n - 1 + 2 * core, n), across]
    biases = []
    for block in ids:
        hit = jnp.int32(0)
        for j in range(NBR_MAX):
            hit = hit + jnp.where((nbr[0, j] == block) & (j < cnt[0]), 1, 0)
        biases.append(jnp.full((1, BLOCK), jnp.where(hit > 0, 0.0, NEG), F32))
    biases.append(jnp.zeros((1, BLOCK), F32))
    bias = jnp.concatenate(biases, axis=1)

    def chunk(j, carry):
        hop_mate(j).wait_recv()
        hop_last(j).wait_recv()

        def spatial(k, inner):
            t = j * per_chunk + k
            kv[t, pl.ds(0, got), :] = dot(win[t, pl.ds(0, got), :], swkv[...]).astype(BF16)
            for p in range(parts):
                lanes = slice(p * LANES, (p + 1) * LANES)
                ctx[k, :, lanes] = attend(
                    q[t, :, lanes], kv[t, :, lanes],
                    kv[t, :, width + p * LANES : width + (p + 1) * LANES], bias,
                )
            return inner

        lax.fori_loop(0, per_chunk, spatial, 0)

        @pl.when(j + 1 < CHUNKS)
        def _():
            relay(j + 1)

        spaced = jnp.concatenate(
            [
                jnp.concatenate(
                    [
                        mixed[side, p, pl.ds(j * per_chunk + k, BLOCK, stride=steps), :]
                        for p in range(parts)
                    ],
                    axis=1,
                )
                for k in range(per_chunk)
            ],
            axis=0,
        )
        after = (spaced + dot(ctx[...].reshape(per_chunk * BLOCK, width), swo[...])).astype(BF16)
        after = after.astype(F32)
        mn = norm(after, g_mlp[...])
        total = after
        hidden_width = gate.shape[1]
        piece = min(512, hidden_width)
        for f in range(0, hidden_width, piece):
            v = dot(mn, gate[:, f : f + piece])
            u = dot(mn, up[:, f : f + piece])
            hidden = ((0.5 * v) * (1.0 + jnp.tanh(0.5 * v)) * u).astype(BF16)
            total = total + dot(hidden, down[f : f + piece, :])
        for k in range(per_chunk):
            for p in range(parts):
                outf[p, pl.ds(j * per_chunk + k, BLOCK, stride=steps), :] = total[
                    k * BLOCK : (k + 1) * BLOCK, p * LANES : (p + 1) * LANES
                ]
        return carry

    lax.fori_loop(0, CHUNKS, chunk, 0)

    for p in range(parts):
        out[:, p * LANES : (p + 1) * LANES] = outf[p].astype(BF16)

    def drain(d, carry):
        to_peer(d).wait_send()
        return carry

    lax.fori_loop(1, half, drain, 0)

    def drain_across(e, carry):
        pass_across(e).wait_send()
        return carry

    lax.fori_loop(0, GROUPS, drain_across, 0)

    def drain_hops(j, carry):
        hop_onward(j).wait_send()
        hop_mate(j).wait_send()
        hop_last(j).wait_send()
        return carry

    lax.fori_loop(0, CHUNKS, drain_hops, 0)


def per_device(
    frames, norm_time, t_wq, t_wkv, t_wo, norm_space, s_wq, s_wkv, s_wo, norm_mlp,
    w_gate, w_up, w_down, nbr_blocks, nbr_count,
):
    n = lax.axis_size("cell")
    cells, steps, width = frames.shape
    rows = cells * steps
    hidden = w_gate.shape[1]
    parts = width // LANES
    smem = pl.BlockSpec(memory_space=pltpu.SMEM)
    vmem = pl.BlockSpec(memory_space=pltpu.VMEM)
    anyw = pl.BlockSpec(memory_space=pl.ANY)
    weights = [t_wq, t_wkv, t_wo, s_wq, s_wkv, s_wo, w_gate, w_up, w_down]
    out = pl.pallas_call(
        functools.partial(layer, n, steps),
        out_shape=jax.ShapeDtypeStruct((rows, width), BF16),
        in_specs=[smem, smem, vmem, vmem, vmem, anyw] + [anyw] * len(weights),
        out_specs=vmem,
        scratch_shapes=[
            pltpu.VMEM((2, n // 4, 2, 2, rows // n, width), BF16),
            pltpu.VMEM((2, parts, rows, LANES), F32),
            pltpu.VMEM((steps, 5 * BLOCK, width), BF16),
            pltpu.VMEM((steps, BLOCK, width), BF16),
            pltpu.VMEM((steps, 5 * BLOCK, 2 * width), BF16),
            pltpu.VMEM((steps // CHUNKS, BLOCK, width), BF16),
            pltpu.VMEM((parts, rows, LANES), F32),
        ]
        + [pltpu.VMEM(w.shape, BF16) for w in weights]
        + [
            pltpu.SemaphoreType.DMA((len(weights),)),
            pltpu.SemaphoreType.DMA,
            pltpu.SemaphoreType.DMA((n // 2,)),
            pltpu.SemaphoreType.DMA((n // 2,)),
            pltpu.SemaphoreType.DMA((GROUPS,)),
            pltpu.SemaphoreType.DMA((GROUPS,)),
            pltpu.SemaphoreType.DMA((3, CHUNKS)),
            pltpu.SemaphoreType.DMA((3, CHUNKS)),
        ],
        compiler_params=pltpu.CompilerParams(
            collective_id=0, has_side_effects=True, vmem_limit_bytes=56 * 1024 * 1024
        ),
        cost_estimate=pl.CostEstimate(
            flops=2 * rows * width * (12 * width + 3 * hidden), bytes_accessed=14 * 2**20,
            transcendentals=rows * 5 * BLOCK * HEADS,
        ),
    )(
        nbr_blocks, nbr_count, norm_time[None], norm_space[None], norm_mlp[None],
        frames.reshape(n // 4, 2, 2, rows // n, width), *weights,
    )
    return out.reshape(cells, steps, width)


def solution(mesh):
    split3 = P(("groups", "cell"), None, None)
    placed = (split3,) + (P(),) * 12 + (P(("groups", "cell"), None), P(("groups", "cell")))
    return jax.shard_map(
        per_device, mesh=mesh, in_specs=placed, out_specs=split3, check_vma=False
    )
```
